128 devices in a mesh: row: 8 (over z, core), col: 16 (over x, y).
Axes of the slice: x: 4, y: 4, z: 4, core: 2. Of those that a mesh axis runs over, the one named last changes fastest.
Arguments:
- pencil_a: float32 [8, 1536, 16, 768], P('row', None, 'col'), may hold values from -6 to 6, as said below
- pencil_b: float32 [8, 1536, 16, 768], P('row', None, 'col'), may hold values from -6 to 6
Outputs:
- new_a: float32 [8, 1536, 16, 768], P('row', None, 'col')
- new_b: float32 [8, 1536, 16, 768], P('row', None, 'col')
The draws below stay inside these ranges and needn't reach their ends.
Inputs may be any that keep to these rules, and one draw needn't show every extreme that they name: `pencil_a`: the first 256 columns of Amat are zero in the last 256 rows of Amat.
All inputs are finite; a program needn't handle non-finite values.
Results may differ from the reference program's by a relative error of at most 0.000056.
Values sent between devices are 32-bit elements; how exact they have to be, the bound alone decides.
No kernel may reach another device: no remote copies, remote signals or barrier semaphores. Data moves between devices by JAX's collectives and lax.ppermute only.
A program may use at most 128 MiB of HBM per device.

```python
import math
import jax
import jax.numpy as jnp
from jax import lax

N = 12288
NB = 256
N_ROW = 8
N_COL = 16


decay_ratio = 3.0


def to_storage(matrix):
    six = matrix.reshape(N // (NB * N_ROW), N_ROW, NB, N // (NB * N_COL), N_COL, NB)
    return six.transpose(1, 0, 2, 4, 3, 5).reshape(N_ROW, N // N_ROW, N_COL, N // N_COL)


def base_field(key):
    return jax.random.normal(key, (N, N), jnp.float32)


def decay_scales():
    fraction = jnp.arange(NB, dtype=jnp.float32) / (NB - 1)
    return jnp.exp(-math.log(decay_ratio) * fraction)


def reflect_columns(block, key):
    direction = jax.random.normal(key, (NB,), jnp.float32)
    direction = direction / jnp.sqrt(jnp.sum(direction * direction))
    along = jnp.dot(block, direction, precision=lax.Precision.HIGHEST)
    return block - 2.0 * jnp.outer(along, direction)


def draw_pencil_a(key, part):
    inner_key = jax.random.fold_in(key, 11)
    field_key, first_key, second_key = jax.random.split(inner_key, 3)
    matrix = base_field(field_key)
    panel = matrix[:, :NB] * decay_scales()[None, :]
    panel = reflect_columns(panel, first_key)
    panel = reflect_columns(panel, second_key)
    kept_rows = (jnp.arange(N) < N - NB).astype(jnp.float32)[:, None]
    matrix = matrix.at[:, :NB].set(panel * kept_rows)
    return to_storage(jnp.clip(matrix, -6.0, 6.0))


def draw_pencil_b(key, part):
    inner_key = jax.random.fold_in(key, 23)
    field_key, first_key, second_key = jax.random.split(inner_key, 3)
    matrix = base_field(field_key)
    strip_rows = matrix[N - NB:, :] * decay_scales()[:, None]
    mixed_t = reflect_columns(strip_rows.T, first_key)
    mixed_t = reflect_columns(mixed_t, second_key)
    matrix = matrix.at[N - NB:, :].set(mixed_t.T)
    return to_storage(jnp.clip(matrix, -6.0, 6.0))


def setup_inputs(seed: int = 0) -> dict:
    key_list = jax.random.split(jax.random.key(seed), 3)
    pencil_a = draw_pencil_a(jax.random.fold_in(key_list[2], 71), 0)
    pencil_b = draw_pencil_b(jax.random.fold_in(key_list[2], 71), 0)
    return dict(pencil_a=pencil_a, pencil_b=pencil_b)


def matmul(left, right):
    return jnp.dot(left.astype(jnp.float32), right.astype(jnp.float32), precision=lax.Precision.HIGHEST, preferred_element_type=jnp.float32)

def inverse_factor(gram):
    lower = jnp.linalg.cholesky(gram)
    ident = jnp.eye(gram.shape[0], dtype=jnp.float32)
    return jax.scipy.linalg.solve_triangular(lower, ident, lower=True).T

def general_inverse(square):
    lower = jnp.linalg.cholesky(matmul(square, square.T))
    ident = jnp.eye(square.shape[0], dtype=jnp.float32)
    linv = jax.scipy.linalg.solve_triangular(lower, ident, lower=True)
    return matmul(square.T, matmul(linv.T, linv))

def to_matrix(stored):
    six = stored.reshape(N_ROW, N // (NB * N_ROW), NB, N_COL, N // (NB * N_COL), NB)
    return six.transpose(1, 0, 2, 4, 3, 5).reshape(N, N)

def to_stored(matrix):
    six = matrix.reshape(N // (NB * N_ROW), N_ROW, NB, N // (NB * N_COL), N_COL, NB)
    return six.transpose(1, 0, 2, 4, 3, 5).reshape(N_ROW, N // N_ROW, N_COL, N // N_COL)

def reference(pencil_a, pencil_b):
    amat = to_matrix(pencil_a)
    bmat = to_matrix(pencil_b)
    ident = jnp.eye(NB, dtype=jnp.float32)
    panel = amat[:, :NB]
    first_inv = inverse_factor(matmul(panel.T, panel))
    basis = matmul(panel, first_inv)
    kinv_left = general_inverse(ident + basis[:NB])
    vectors = basis.at[:NB].add(ident)
    amat = amat - matmul(vectors, matmul(kinv_left, matmul(vectors.T, amat)))
    bmat = bmat - matmul(vectors, matmul(kinv_left, matmul(vectors.T, bmat)))
    strip = bmat[N - NB:]
    first_inv = inverse_factor(matmul(strip, strip.T))
    basis_t = matmul(first_inv.T, strip)
    kinv_right = general_inverse(ident + basis_t[:, N - NB:].T)
    vectors_t = basis_t.at[:, N - NB:].add(ident)
    amat = amat - matmul(matmul(matmul(amat, vectors_t.T), kinv_right.T), vectors_t)
    bmat = bmat - matmul(matmul(matmul(bmat, vectors_t.T), kinv_right.T), vectors_t)
    return (to_stored(amat), to_stored(bmat))
```

```python
import jax
import jax.numpy as jnp
from jax import lax
from jax.experimental import pallas as pl
from jax.experimental.pallas import tpu as pltpu
from jax.sharding import PartitionSpec as P

NB = 256
LEAF = 64


def dot(a, b, ca=1, cb=0):
    return lax.dot_general(a, b, (((ca,), (cb,)), ((), ())), precision=lax.Precision.HIGHEST,
                           preferred_element_type=jnp.float32)

PB = 4

def leaf_inverse(tiles, forward):
    n = len(tiles)
    wide = (8, 2 * LEAF)
    rows = lax.broadcasted_iota(jnp.int32, (LEAF, LEAF), 0)
    cols = lax.broadcasted_iota(jnp.int32, (LEAF, LEAF), 1)
    eye = (rows == cols).astype(jnp.float32)
    row_id = lax.broadcasted_iota(jnp.int32, wide, 0)
    full = [jnp.concatenate([t, eye], axis=1) for t in tiles]
    groups = LEAF // 8
    work = [[f[8 * g : 8 * g + 8] for g in range(groups)] for f in full]
    for j in range(0, LEAF, PB):
        own, at = j // 8, j % 8
        for m in range(n):
            w = work[m]
            touched = range(own, groups) if forward else range(groups)
            columns = {g: [jnp.broadcast_to(w[g][:, j + b : j + b + 1], wide) for b in range(PB)] for g in touched}
            band = [jnp.broadcast_to(w[own][at + a : at + a + 1, :], wide) for a in range(PB)]
            d = [[jnp.broadcast_to(columns[own][b][at + a : at + a + 1, :], wide) for b in range(PB)] for a in range(PB)]
            inv = []
            for k in range(PB):
                inv.append(1.0 / d[k][k])
                for a in range(k + 1, PB):
                    ratio = d[a][k] * inv[k]
                    for b in range(k + 1, PB):
                        d[a][b] = d[a][b] - ratio * d[k][b]
                    band[a] = band[a] - ratio * band[k]
            solved = list(band)
            if not forward:
                for a in reversed(range(PB)):
                    for b in range(a + 1, PB):
                        solved[a] = solved[a] - d[a][b] * solved[b]
                    solved[a] = solved[a] * inv[a]
            for g in touched:
                total = w[g]
                c = []
                for b in range(PB):
                    v = columns[g][b]
                    for k in range(b):
                        v = v - c[k] * d[k][b]
                    c.append(v * inv[b])
                    total = total - c[b] * band[b]
                if g == own:
                    if forward:
                        total = jnp.where(row_id < at, w[g], total)
                    for a in range(PB):
                        total = jnp.where(row_id == at + a, solved[a], total)
                w[g] = total
    out = []
    for m in range(n):
        f = jnp.concatenate(work[m], axis=0)
        left, right = f[:, :LEAF], f[:, LEAF:]
        if forward:
            dd = jnp.sum(jnp.where(rows == cols, left, 0.0), axis=1, keepdims=True)
            right = right * lax.rsqrt(dd)
        out.append(right)
    return out

def factor_kernel(g_ref, e_ref, linv_ref, m_ref, w_ref):
    n = g_ref.shape[0]
    rows = lax.broadcasted_iota(jnp.int32, (NB, NB), 0)
    cols = lax.broadcasted_iota(jnp.int32, (NB, NB), 1)
    eye = (rows == cols).astype(jnp.float32)
    steps = NB // LEAF
    for m in range(n):
        w_ref[m, :, :NB] = g_ref[m]
        w_ref[m, :, NB:] = eye
    for k in range(steps):
        lo, hi = k * LEAF, (k + 1) * LEAF
        inv = leaf_inverse([w_ref[m, lo:hi, lo:hi] for m in range(n)], True)
        for m in range(n):
            band = dot(inv[m], w_ref[m, lo:hi, :])
            w_ref[m, lo:hi, :] = band
            if k < steps - 1:
                w_ref[m, hi:, :] = w_ref[m, hi:, :] - dot(band[:, hi:NB], band, 0, 0)
    for m in range(n):
        linv = w_ref[m, :, NB:]
        linv_ref[m] = linv
        w_ref[m, :, :NB] = eye + dot(e_ref[m], linv, 1, 1)
        w_ref[m, :, NB:] = eye
    for k in range(steps):
        lo, hi = k * LEAF, (k + 1) * LEAF
        inv = leaf_inverse([w_ref[m, lo:hi, lo:hi] for m in range(n)], False)
        for m in range(n):
            band = dot(inv[m], w_ref[m, lo:hi, :])
            whole = w_ref[m]
            w_ref[m] = whole - dot(whole[:, lo:hi], band)
            w_ref[m, lo:hi, :] = band
    for m in range(n):
        m_ref[m] = w_ref[m, :, NB:]

def factor(g, e):
    n = g.shape[0]
    return pl.pallas_call(
        factor_kernel,
        out_shape=(jax.ShapeDtypeStruct((n, NB, NB), jnp.float32),) * 2,
        in_specs=[pl.BlockSpec(memory_space=pltpu.VMEM)] * 2,
        out_specs=(pl.BlockSpec(memory_space=pltpu.VMEM),) * 2,
        scratch_shapes=[pltpu.VMEM((n, NB, 2 * NB), jnp.float32)],
        compiler_params=pltpu.CompilerParams(vmem_limit_bytes=32 * 2**20),
        cost_estimate=pl.CostEstimate(flops=2 * 10**9, bytes_accessed=2 * 10**6, transcendentals=0),
    )(g, e)


def matmul(left, right, dims=((1,), (0,)), precision=lax.Precision.HIGH):
    return lax.dot_general(left, right, (dims, ((), ())), precision=precision, preferred_element_type=jnp.float32)


def reduced_part(array, axis):
    count = lax.axis_size(axis)
    parts = lax.all_to_all(array.reshape(count, -1, array.shape[1]), axis, 0, 0, tiled=True)
    return jnp.sum(parts, axis=0)


def joined(part, axis):
    return lax.all_gather(part, axis, tiled=True)


def from_root(array, axis, root):
    count = lax.axis_size(axis)
    parts = lax.all_to_all(array.reshape(count, -1, array.shape[1]), axis, 0, 0, tiled=True)
    return joined(parts[root], axis)


def on_device(pencil_a, pencil_b):
    rows_loc = pencil_a.shape[1]
    cols_loc = pencil_a.shape[3]
    amat = pencil_a.reshape(rows_loc, cols_loc)
    bmat = pencil_b.reshape(rows_loc, cols_loc)
    row, col = lax.axis_index("row"), lax.axis_index("col")
    last_row = lax.axis_size("row") - 1
    last_col = lax.axis_size("col") - 1
    is_top, is_end = row == 0, col == last_col
    exact = lax.Precision.HIGHEST
    panel = amat[:, :NB]
    strip = bmat[rows_loc - NB :]
    gram_l = matmul(panel, panel, ((0,), (0,)), exact)
    gram_r = matmul(strip, strip, ((1,), (1,)), exact)
    end_t = strip[:, cols_loc - NB :].T
    in_panel, in_strip = col == 0, row == last_row
    small = jnp.concatenate(
        [
            jnp.where(in_panel, gram_l, 0.0),
            jnp.where(in_panel & is_top, panel[:NB], 0.0),
            jnp.where(in_strip, gram_r, 0.0),
            jnp.where(in_strip & is_end, end_t, 0.0),
        ]
    )
    small = reduced_part(reduced_part(small, "row"), "col")
    small = joined(joined(small, "col"), "row").reshape(2, 2, NB, NB)
    linv, minv = factor(small[:, 0], small[:, 1])
    panel = from_root(panel, "col", 0)
    strip = from_root(strip, "row", last_row)
    unit = jnp.eye(NB, dtype=jnp.float32)
    vectors = matmul(panel, linv[0], ((1,), (1,)))
    vectors = vectors + jnp.where(is_top, jnp.pad(unit, ((0, rows_loc - NB), (0, 0))), 0.0)
    vectors_t = matmul(linv[1], strip)
    vectors_t = vectors_t + jnp.where(is_end, jnp.pad(unit, ((0, 0), (cols_loc - NB, 0))), 0.0)
    both = ((0,), (0,))
    left = jnp.concatenate([matmul(vectors, amat, both), matmul(vectors, bmat, both)], axis=1)
    across = ((1,), (1,))
    right = jnp.concatenate([matmul(amat, vectors_t, across), matmul(bmat, vectors_t, across)])
    right = reduced_part(right, "col")
    left = reduced_part(left, "row")
    right = joined(matmul(right, minv[1], across), "col")
    left = matmul(minv[0], joined(left, "row"))
    cross = jnp.concatenate(
        [matmul(left[:, :cols_loc], vectors_t, across), matmul(left[:, cols_loc:], vectors_t, across)]
    )
    cross = joined(reduced_part(cross, "col"), "col")
    cross = matmul(cross, minv[1], across)
    out = []
    for i, mat in enumerate((amat, bmat)):
        mine = left[:, i * cols_loc : (i + 1) * cols_loc] - matmul(cross[i * NB : (i + 1) * NB], vectors_t)
        mixed = right[i * rows_loc : (i + 1) * rows_loc]
        mat = mat - matmul(
            jnp.concatenate([vectors, mixed], axis=1), jnp.concatenate([mine, vectors_t], axis=0)
        )
        out.append(mat.reshape(1, rows_loc, 1, cols_loc))
    return tuple(out)


def solution(mesh):
    placed = (P("row", None, "col", None), P("row", None, "col", None))
    return jax.shard_map(on_device, mesh=mesh, in_specs=placed, out_specs=placed, check_vma=False)
```

```python
import jax
import jax.numpy as jnp
from jax import lax
from jax.experimental import pallas as pl
from jax.experimental.pallas import tpu as pltpu
from jax.sharding import PartitionSpec as P

NB = 256
LEAF = 64
LANES = 128
TILE = 256
VMEM = pl.BlockSpec(memory_space=pltpu.VMEM)


def dot(a, b, ca=1, cb=0):
    return lax.dot_general(a, b, (((ca,), (cb,)), ((), ())), precision=lax.Precision.HIGHEST,
                           preferred_element_type=jnp.float32)

PB = 4

def leaf_inverse(tiles, forward):
    n = len(tiles)
    wide = (8, 2 * LEAF)
    rows = lax.broadcasted_iota(jnp.int32, (LEAF, LEAF), 0)
    cols = lax.broadcasted_iota(jnp.int32, (LEAF, LEAF), 1)
    eye = (rows == cols).astype(jnp.float32)
    row_id = lax.broadcasted_iota(jnp.int32, wide, 0)
    full = [jnp.concatenate([t, eye], axis=1) for t in tiles]
    groups = LEAF // 8
    work = [[f[8 * g : 8 * g + 8] for g in range(groups)] for f in full]
    for j in range(0, LEAF, PB):
        own, at = j // 8, j % 8
        for m in range(n):
            w = work[m]
            touched = range(own, groups) if forward else range(groups)
            columns = {g: [jnp.broadcast_to(w[g][:, j + b : j + b + 1], wide) for b in range(PB)] for g in touched}
            band = [jnp.broadcast_to(w[own][at + a : at + a + 1, :], wide) for a in range(PB)]
            d = [[jnp.broadcast_to(columns[own][b][at + a : at + a + 1, :], wide) for b in range(PB)] for a in range(PB)]
            inv = []
            for k in range(PB):
                inv.append(1.0 / d[k][k])
                for a in range(k + 1, PB):
                    ratio = d[a][k] * inv[k]
                    for b in range(k + 1, PB):
                        d[a][b] = d[a][b] - ratio * d[k][b]
                    band[a] = band[a] - ratio * band[k]
            solved = list(band)
            if not forward:
                for a in reversed(range(PB)):
                    for b in range(a + 1, PB):
                        solved[a] = solved[a] - d[a][b] * solved[b]
                    solved[a] = solved[a] * inv[a]
            for g in touched:
                total = w[g]
                c = []
                for b in range(PB):
                    v = columns[g][b]
                    for k in range(b):
                        v = v - c[k] * d[k][b]
                    c.append(v * inv[b])
                    total = total - c[b] * band[b]
                if g == own:
                    if forward:
                        total = jnp.where(row_id < at, w[g], total)
                    for a in range(PB):
                        total = jnp.where(row_id == at + a, solved[a], total)
                w[g] = total
    out = []
    for m in range(n):
        f = jnp.concatenate(work[m], axis=0)
        left, right = f[:, :LEAF], f[:, LEAF:]
        if forward:
            dd = jnp.sum(jnp.where(rows == cols, left, 0.0), axis=1, keepdims=True)
            right = right * lax.rsqrt(dd)
        out.append(right)
    return out

def lower_kernel(left_ref, right_ref, out_ref, w_ref):
    rows = lax.broadcasted_iota(jnp.int32, (NB, NB), 0)
    cols = lax.broadcasted_iota(jnp.int32, (NB, NB), 1)
    sides = (left_ref, right_ref)
    steps = NB // LEAF
    for m, ref in enumerate(sides):
        w_ref[m, :, :NB] = ref[:NB, :]
        w_ref[m, :, NB:] = (rows == cols).astype(jnp.float32)
    for k in range(steps):
        lo, hi = k * LEAF, (k + 1) * LEAF
        inv = leaf_inverse([w_ref[m, lo:hi, lo:hi] for m in range(2)], True)
        for m in range(2):
            band = dot(inv[m], w_ref[m, lo:hi, :])
            w_ref[m, lo:hi, :] = band
            if k < steps - 1:
                w_ref[m, hi:, :] = w_ref[m, hi:, :] - dot(band[:, hi:NB], band, 0, 0)
    for m in range(2):
        out_ref[m] = w_ref[m, :, NB:]


def general_kernel(left_ref, right_ref, linv_ref, out_ref, w_ref):
    rows = lax.broadcasted_iota(jnp.int32, (NB, NB), 0)
    cols = lax.broadcasted_iota(jnp.int32, (NB, NB), 1)
    eye = (rows == cols).astype(jnp.float32)
    for m, ref in enumerate((left_ref, right_ref)):
        w_ref[m, :, :NB] = eye + dot(ref[NB:, :], linv_ref[m], 1, 1)
        w_ref[m, :, NB:] = eye
    for k in range(NB // LEAF):
        lo, hi = k * LEAF, (k + 1) * LEAF
        inv = leaf_inverse([w_ref[m, lo:hi, lo:hi] for m in range(2)], False)
        for m in range(2):
            band = dot(inv[m], w_ref[m, lo:hi, :])
            whole = w_ref[m]
            w_ref[m] = whole - dot(whole[:, lo:hi], band)
            w_ref[m, lo:hi, :] = band
    for m in range(2):
        out_ref[m] = w_ref[m, :, NB:]


def lower_inverses(left, right):
    return pl.pallas_call(
        lower_kernel,
        out_shape=jax.ShapeDtypeStruct((2, NB, NB), jnp.float32),
        in_specs=[VMEM] * 2,
        out_specs=VMEM,
        scratch_shapes=[pltpu.VMEM((2, NB, 2 * NB), jnp.float32)],
        compiler_params=pltpu.CompilerParams(vmem_limit_bytes=24 * 2**20),
        cost_estimate=pl.CostEstimate(flops=2 * 10**10, bytes_accessed=2 * 10**6, transcendentals=0),
    )(left, right)


def general_inverses(left, right, linv):
    return pl.pallas_call(
        general_kernel,
        out_shape=jax.ShapeDtypeStruct((2, NB, NB), jnp.float32),
        in_specs=[VMEM] * 3,
        out_specs=VMEM,
        scratch_shapes=[pltpu.VMEM((2, NB, 2 * NB), jnp.float32)],
        compiler_params=pltpu.CompilerParams(vmem_limit_bytes=24 * 2**20),
        cost_estimate=pl.CostEstimate(flops=2 * 10**10, bytes_accessed=2 * 10**6, transcendentals=0),
    )(left, right, linv)


def halves(x):
    high = x.astype(jnp.bfloat16)
    return high, (x - high.astype(jnp.float32)).astype(jnp.bfloat16)


def dot3(a, b, ca=1, cb=0):
    dims = (((ca,), (cb,)), ((), ()))

    def one(left, right):
        return lax.dot_general(left, right, dims, preferred_element_type=jnp.float32)

    return one(a[0], b[0]) + (one(a[0], b[1]) + one(a[1], b[0]))


def rows_of(ref, width, first=0, count=None):
    count = width if count is None else count
    height = ref.shape[0] // width
    return jnp.concatenate([ref[pl.ds(first + t, height, stride=width), :] for t in range(count)], axis=1)


def gram_kernel(flags_ref, a_ref, b_ref, panel_ref, strip_ref, left_ref, right_ref):
    i = pl.program_id(0)
    width = strip_ref.shape[1] // LANES
    panel = rows_of(a_ref, width, 0, NB // LANES)
    panel_ref[...] = panel
    gram = dot(panel, panel, 0, 0)

    @pl.when(i == 0)
    def _():
        left_ref[:NB, :] = gram
        left_ref[NB:, :] = jnp.where(flags_ref[0] == 1, panel[:NB], 0.0)

    @pl.when(i > 0)
    def _():
        left_ref[:NB, :] += gram

    @pl.when(i == pl.num_programs(0) - 1)
    def _():
        strip = rows_of(b_ref, width)
        strip_ref[...] = strip
        right_ref[:NB, :] = dot(strip, strip, 1, 1)
        right_ref[NB:, :] = jnp.where(flags_ref[1] == 1, strip[:, strip.shape[1] - NB :].T, 0.0)


def grams(flags, araw, braw, rows_loc, cols_loc):
    width = cols_loc // LANES
    steps = rows_loc // TILE
    f32 = jnp.float32
    return pl.pallas_call(
        gram_kernel,
        out_shape=(
            jax.ShapeDtypeStruct((rows_loc, NB), f32),
            jax.ShapeDtypeStruct((NB, cols_loc), f32),
            jax.ShapeDtypeStruct((2 * NB, NB), f32),
            jax.ShapeDtypeStruct((2 * NB, NB), f32),
        ),
        grid_spec=pltpu.PrefetchScalarGridSpec(
            num_scalar_prefetch=1,
            grid=(steps,),
            in_specs=[
                pl.BlockSpec((TILE * width, LANES), lambda i, f: (i, 0)),
                pl.BlockSpec((NB * width, LANES), lambda i, f: (rows_loc // NB - 1, 0)),
            ],
            out_specs=[
                pl.BlockSpec((TILE, NB), lambda i, f: (i, 0)),
                pl.BlockSpec((NB, cols_loc), lambda i, f: (0, 0)),
                pl.BlockSpec((2 * NB, NB), lambda i, f: (0, 0)),
                pl.BlockSpec((2 * NB, NB), lambda i, f: (0, 0)),
            ],
        ),
        compiler_params=pltpu.CompilerParams(vmem_limit_bytes=32 * 2**20),
        cost_estimate=pl.CostEstimate(flops=2 * 10**9, bytes_accessed=6 * 10**6, transcendentals=0),
    )(flags, araw, braw)


def product_kernel(a_ref, b_ref, panel_ref, strip_ref, left_ref, right_ref, top_ref, end_ref, s_ref):
    i = pl.program_id(0)
    cols_loc = strip_ref.shape[1]
    width = cols_loc // LANES

    @pl.when(i == 0)
    def _():
        high, low = halves(strip_ref[...])
        s_ref[0] = high
        s_ref[1] = low

    strip = (s_ref[0], s_ref[1])
    panel = halves(panel_ref[...])
    for m, ref in enumerate((a_ref, b_ref)):
        whole = rows_of(ref, width)
        x = halves(whole)
        right_ref[m] = dot3(x, strip, 1, 1)
        end_ref[m] = whole[:, cols_loc - NB :]
        part = dot3(panel, x, 0, 0)
        at = slice(m * cols_loc, (m + 1) * cols_loc)

        @pl.when(i == 0)
        def _():
            left_ref[:, at] = part
            top_ref[:, at] = whole[:NB]

        @pl.when(i > 0)
        def _():
            left_ref[:, at] += part


def products(araw, braw, panel, strip):
    rows_loc, cols_loc = panel.shape[0], strip.shape[1]
    width = cols_loc // LANES
    f32 = jnp.float32
    raw = pl.BlockSpec((TILE * width, LANES), lambda i: (i, 0))
    wide = pl.BlockSpec((NB, 2 * cols_loc), lambda i: (0, 0))
    tall = pl.BlockSpec((2, TILE, NB), lambda i: (0, i, 0))
    return pl.pallas_call(
        product_kernel,
        grid=(rows_loc // TILE,),
        out_shape=(
            jax.ShapeDtypeStruct((NB, 2 * cols_loc), f32),
            jax.ShapeDtypeStruct((2, rows_loc, NB), f32),
            jax.ShapeDtypeStruct((NB, 2 * cols_loc), f32),
            jax.ShapeDtypeStruct((2, rows_loc, NB), f32),
        ),
        in_specs=[raw, raw, pl.BlockSpec((TILE, NB), lambda i: (i, 0)), pl.BlockSpec((NB, cols_loc), lambda i: (0, 0))],
        out_specs=(wide, tall, wide, tall),
        scratch_shapes=[pltpu.VMEM((2, NB, cols_loc), jnp.bfloat16)],
        compiler_params=pltpu.CompilerParams(vmem_limit_bytes=48 * 2**20),
        cost_estimate=pl.CostEstimate(flops=75 * 10**8, bytes_accessed=24 * 10**6, transcendentals=0),
    )(araw, braw, panel, strip)


def update_kernel(flags_ref, a_ref, b_ref, panel_ref, mixed_ref, lift_ref, top_ref, strip_ref, oa_ref, ob_ref, w_ref):
    i = pl.program_id(0)
    cols_loc = strip_ref.shape[1]
    width = cols_loc // LANES

    @pl.when(i == 0)
    def _():
        zh, zl = halves(strip_ref[...])
        lh, ll = halves(lift_ref[...])
        for m in range(2):
            at = slice(m * cols_loc, (m + 1) * cols_loc)
            w_ref[0, m, :NB, :] = lh[:, at]
            w_ref[1, m, :NB, :] = ll[:, at]
            w_ref[0, m, NB:, :] = zh
            w_ref[1, m, NB:, :] = zl

    panel = panel_ref[...]
    on_top = (i == 0) & (flags_ref[0] == 1)
    for m, (ref, out) in enumerate(((a_ref, oa_ref), (b_ref, ob_ref))):
        both = halves(jnp.concatenate([panel, mixed_ref[m]], axis=1))
        delta = dot3(both, (w_ref[0, m], w_ref[1, m]))
        for t in range(width):
            lanes = slice(t * LANES, (t + 1) * LANES)
            line = pl.ds(t, TILE, stride=width)
            out[line, :] = ref[line, :] - delta[:, lanes]

        @pl.when(on_top)
        def _():
            for t in range(width):
                line = pl.ds(t, NB, stride=width)
                lanes = slice(m * cols_loc + t * LANES, m * cols_loc + (t + 1) * LANES)
                out[line, :] = out[line, :] - top_ref[:, lanes]


def updated(flags, araw, braw, panel, mixed, lift, top, vectors_t):
    rows_loc, cols_loc = panel.shape[0], vectors_t.shape[1]
    width = cols_loc // LANES
    raw = pl.BlockSpec((TILE * width, LANES), lambda i, f: (i, 0))
    wide = pl.BlockSpec((NB, 2 * cols_loc), lambda i, f: (0, 0))
    return pl.pallas_call(
        update_kernel,
        out_shape=(jax.ShapeDtypeStruct(araw.shape, jnp.float32),) * 2,
        grid_spec=pltpu.PrefetchScalarGridSpec(
            num_scalar_prefetch=1,
            grid=(rows_loc // TILE,),
            in_specs=[
                raw,
                raw,
                pl.BlockSpec((TILE, NB), lambda i, f: (i, 0)),
                pl.BlockSpec((2, TILE, NB), lambda i, f: (0, i, 0)),
                wide,
                wide,
                pl.BlockSpec((NB, cols_loc), lambda i, f: (0, 0)),
            ],
            out_specs=[raw, raw],
            scratch_shapes=[pltpu.VMEM((2, 2, 2 * NB, cols_loc), jnp.bfloat16)],
        ),
        compiler_params=pltpu.CompilerParams(vmem_limit_bytes=48 * 2**20),
        cost_estimate=pl.CostEstimate(flops=75 * 10**8, bytes_accessed=28 * 10**6, transcendentals=0),
    )(flags, araw, braw, panel, mixed, lift, top, vectors_t)


Z, CORE, X, Y = ("row", 2, 4), ("row", 1, 2), ("col", 4, 4), ("col", 1, 4)


def place(ring):
    axis, stride, size = ring
    return lax.rem(lax.axis_index(axis) // stride, size)


def pairs(ring, shift, root=None, others=None):
    axis, stride, size = ring
    out = []
    for i in range(lax.axis_size(axis)):
        p = (i // stride) % size
        if root is not None and p != root:
            continue
        if others is not None and i - p * stride not in others:
            continue
        out.append((i, i + ((p + shift) % size - p) * stride))
    return out


def shifted(array, ring, shift, root=None, others=None):
    return lax.ppermute(array, ring[0], pairs(ring, shift, root, others))


def at(array, index):
    return lax.dynamic_index_in_dim(array, index, 0, keepdims=False)


def ring_part(array, ring):
    size = ring[2]
    parts = array.reshape(size, -1, array.shape[-1])
    me = place(ring)
    total = at(parts, me)
    for s in range(1, size):
        total = total + shifted(at(parts, lax.rem(me + s, size)), ring, s)
    return total


def ring_join(part, ring):
    size = ring[2]
    me = place(ring)
    got = [shifted(part, ring, s) for s in range(size - 1, 0, -1)] + [part]
    start = lax.rem(size - 1 - me + size, size) * part.shape[0]
    twice = jnp.concatenate(got + got[:-1])
    return lax.dynamic_slice_in_dim(twice, start, size * part.shape[0])


def ring_copy(array, ring, root, others=None):
    total = jnp.where(place(ring) == root, array, 0.0)
    for s in range(1, ring[2]):
        total = total + shifted(array, ring, s, root, others)
    return total


def matmul(left, right, dims=((1,), (0,)), precision=lax.Precision.HIGH):
    return lax.dot_general(left, right, (dims, ((), ())), precision=precision, preferred_element_type=jnp.float32)


def reduced_part(array, axis):
    count = lax.axis_size(axis)
    parts = lax.all_to_all(array.reshape(count, -1, array.shape[1]), axis, 0, 0, tiled=True)
    return jnp.sum(parts, axis=0)


def joined(part, axis):
    return lax.all_gather(part, axis, tiled=True)


def panel_to_all(array):
    count = lax.axis_size("col")
    parts = lax.all_to_all(array.reshape(count, -1, array.shape[1]), "col", 0, 0, tiled=True)
    return joined(parts[0], "col")


def strip_to_all(array):
    core = place(CORE)
    both = array.reshape(2, -1, array.shape[1])
    other = lax.ppermute(both[0], "row", [(7, 6)])
    half = jnp.where(core == 1, both[1], other)
    half = ring_copy(half, Z, 3)
    return ring_join(half, CORE)


def on_device(pencil_a, pencil_b):
    rows_loc = pencil_a.shape[1]
    cols_loc = pencil_a.shape[3]
    araw = pencil_a.reshape(-1, LANES)
    braw = pencil_b.reshape(-1, LANES)
    row, col = lax.axis_index("row"), lax.axis_index("col")
    is_top, is_end = row == 0, col == lax.axis_size("col") - 1
    flags = jnp.stack([is_top, is_end]).astype(jnp.int32)
    across, both = ((1,), (1,)), ((0,), (0,))
    panel, strip, left_sum, right_sum = grams(flags, araw, braw, rows_loc, cols_loc)
    left_sum = ring_part(ring_part(left_sum, CORE), Z)
    left_sum = ring_copy(ring_copy(left_sum, X, 0, (0,)), Y, 0)
    left_sum = ring_join(ring_join(left_sum, Z), CORE)
    right_sum = ring_part(ring_part(right_sum, X), Y)
    right_sum = ring_copy(ring_copy(right_sum, Z, 3, (1,)), CORE, 1)
    right_sum = ring_join(ring_join(right_sum, Y), X)
    linv = lower_inverses(left_sum, right_sum)
    minv = general_inverses(left_sum, right_sum, linv)
    panel = panel_to_all(panel)
    strip = strip_to_all(strip)
    unit = jnp.eye(NB, dtype=jnp.float32)
    left, right, top, end = products(araw, braw, panel, strip)
    right = matmul(right.reshape(2 * rows_loc, NB), linv[1], across)
    right = right + jnp.where(is_end, end.reshape(2 * rows_loc, NB), 0.0)
    right = reduced_part(right, "col")
    left = matmul(linv[0], left) + jnp.where(is_top, top, 0.0)
    left = joined(reduced_part(left, "row"), "row")
    right = joined(matmul(right, minv[1], across), "col")
    vectors_t = matmul(linv[1], strip)
    vectors_t = vectors_t + jnp.where(is_end, jnp.pad(unit, ((0, 0), (cols_loc - NB, 0))), 0.0)
    left = matmul(minv[0], left)
    cross = jnp.concatenate(
        [matmul(left[:, :cols_loc], vectors_t, across), matmul(left[:, cols_loc:], vectors_t, across)]
    )
    cross = ring_join(ring_join(ring_part(ring_part(cross, X), Y), Y), X)
    cross = matmul(matmul(cross, minv[1], across), vectors_t)
    left = left - jnp.concatenate([cross[:NB], cross[NB:]], axis=1)
    lift = matmul(linv[0], left, both)
    new_a, new_b = updated(flags, araw, braw, panel, right.reshape(2, rows_loc, NB), lift, left, vectors_t)
    return new_a.reshape(pencil_a.shape), new_b.reshape(pencil_b.shape)


def solution(mesh):
    placed = (P("row", None, "col", None), P("row", None, "col", None))
    return jax.shard_map(on_device, mesh=mesh, in_specs=placed, out_specs=placed, check_vma=False)
```

```python
import jax
import jax.numpy as jnp
from jax import lax
from jax.experimental import pallas as pl
from jax.experimental.pallas import tpu as pltpu
from jax.sharding import PartitionSpec as P

NB = 256
LEAF = 64
LANES = 128
TILE = 256
N_ROW = 8
N_COL = 16
VMEM = pl.BlockSpec(memory_space=pltpu.VMEM)


def dot(a, b, ca=1, cb=0):
    return lax.dot_general(a, b, (((ca,), (cb,)), ((), ())), precision=lax.Precision.HIGHEST,
                           preferred_element_type=jnp.float32)

PB = 4

def leaf_inverse(tiles, forward):
    n = len(tiles)
    wide = (8, 2 * LEAF)
    rows = lax.broadcasted_iota(jnp.int32, (LEAF, LEAF), 0)
    cols = lax.broadcasted_iota(jnp.int32, (LEAF, LEAF), 1)
    eye = (rows == cols).astype(jnp.float32)
    row_id = lax.broadcasted_iota(jnp.int32, wide, 0)
    full = [jnp.concatenate([t, eye], axis=1) for t in tiles]
    groups = LEAF // 8
    work = [[f[8 * g : 8 * g + 8] for g in range(groups)] for f in full]
    for j in range(0, LEAF, PB):
        own, at = j // 8, j % 8
        for m in range(n):
            w = work[m]
            touched = range(own, groups) if forward else range(groups)
            columns = {g: [jnp.broadcast_to(w[g][:, j + b : j + b + 1], wide) for b in range(PB)] for g in touched}
            band = [jnp.broadcast_to(w[own][at + a : at + a + 1, :], wide) for a in range(PB)]
            d = [[jnp.broadcast_to(columns[own][b][at + a : at + a + 1, :], wide) for b in range(PB)] for a in range(PB)]
            inv = []
            for k in range(PB):
                inv.append(1.0 / d[k][k])
                for a in range(k + 1, PB):
                    ratio = d[a][k] * inv[k]
                    for b in range(k + 1, PB):
                        d[a][b] = d[a][b] - ratio * d[k][b]
                    band[a] = band[a] - ratio * band[k]
            solved = list(band)
            if not forward:
                for a in reversed(range(PB)):
                    for b in range(a + 1, PB):
                        solved[a] = solved[a] - d[a][b] * solved[b]
                    solved[a] = solved[a] * inv[a]
            for g in touched:
                total = w[g]
                c = []
                for b in range(PB):
                    v = columns[g][b]
                    for k in range(b):
                        v = v - c[k] * d[k][b]
                    c.append(v * inv[b])
                    total = total - c[b] * band[b]
                if g == own:
                    if forward:
                        total = jnp.where(row_id < at, w[g], total)
                    for a in range(PB):
                        total = jnp.where(row_id == at + a, solved[a], total)
                w[g] = total
    out = []
    for m in range(n):
        f = jnp.concatenate(work[m], axis=0)
        left, right = f[:, :LEAF], f[:, LEAF:]
        if forward:
            dd = jnp.sum(jnp.where(rows == cols, left, 0.0), axis=1, keepdims=True)
            right = right * lax.rsqrt(dd)
        out.append(right)
    return out

def load(got_ref, m, first, w_ref):
    share = got_ref.shape[1] // 2
    lanes = (1 - m) * share
    for c in range(NB // share):
        w_ref[m, c * share : (c + 1) * share, :NB] = got_ref[first // share + c, lanes : lanes + share, :]


def lower_kernel(got_ref, _, out_ref, w_ref):
    rows = lax.broadcasted_iota(jnp.int32, (NB, NB), 0)
    cols = lax.broadcasted_iota(jnp.int32, (NB, NB), 1)
    steps = NB // LEAF
    for m in range(2):
        load(got_ref, m, 0, w_ref)
        w_ref[m, :, NB:] = (rows == cols).astype(jnp.float32)
    for k in range(steps):
        lo, hi = k * LEAF, (k + 1) * LEAF
        inv = leaf_inverse([w_ref[m, lo:hi, lo:hi] for m in range(2)], True)
        for m in range(2):
            band = dot(inv[m], w_ref[m, lo:hi, :])
            w_ref[m, lo:hi, :] = band
            if k < steps - 1:
                w_ref[m, hi:, :] = w_ref[m, hi:, :] - dot(band[:, hi:NB], band, 0, 0)
    for m in range(2):
        out_ref[m] = w_ref[m, :, NB:]


def general_kernel(got_ref, linv_ref, out_ref, w_ref):
    rows = lax.broadcasted_iota(jnp.int32, (NB, NB), 0)
    cols = lax.broadcasted_iota(jnp.int32, (NB, NB), 1)
    eye = (rows == cols).astype(jnp.float32)
    for m in range(2):
        load(got_ref, m, NB, w_ref)
        w_ref[m, :, :NB] = eye + dot(w_ref[m, :, :NB], linv_ref[m], 1, 1)
        w_ref[m, :, NB:] = eye
    for k in range(NB // LEAF):
        lo, hi = k * LEAF, (k + 1) * LEAF
        inv = leaf_inverse([w_ref[m, lo:hi, lo:hi] for m in range(2)], False)
        for m in range(2):
            band = dot(inv[m], w_ref[m, lo:hi, :])
            whole = w_ref[m]
            w_ref[m] = whole - dot(whole[:, lo:hi], band)
            w_ref[m, lo:hi, :] = band
    for m in range(2):
        out_ref[m] = w_ref[m, :, NB:]


def inverses(kernel, got, other, other_spec):
    return pl.pallas_call(
        kernel,
        out_shape=jax.ShapeDtypeStruct((2, NB, NB), jnp.float32),
        in_specs=[VMEM, other_spec],
        out_specs=VMEM,
        scratch_shapes=[pltpu.VMEM((2, NB, 2 * NB), jnp.float32)],
        compiler_params=pltpu.CompilerParams(vmem_limit_bytes=24 * 2**20),
        cost_estimate=pl.CostEstimate(flops=2 * 10**10, bytes_accessed=2 * 10**6, transcendentals=0),
    )(got, other)


def halves(x):
    high = x.astype(jnp.bfloat16)
    return high, (x - high.astype(jnp.float32)).astype(jnp.bfloat16)


def dot3(a, b, ca=1, cb=0):
    dims = (((ca,), (cb,)), ((), ()))

    def one(left, right):
        return lax.dot_general(left, right, dims, preferred_element_type=jnp.float32)

    return one(a[0], b[0]) + (one(a[0], b[1]) + one(a[1], b[0]))


def rows_of(ref, width, first=0, count=None):
    count = width if count is None else count
    height = ref.shape[0] // width
    return jnp.concatenate([ref[pl.ds(first + t, height, stride=width), :] for t in range(count)], axis=1)


def gram_kernel(flags_ref, a_ref, b_ref, panel_ref, strip_ref, left_ref, right_ref, sum_ref):
    i = pl.program_id(0)
    width = strip_ref.shape[1] // LANES
    panel = rows_of(a_ref, width, 0, NB // LANES)
    panel_ref[...] = panel
    gram = dot(panel, panel, 0, 0)

    @pl.when(i == 0)
    def _():
        sum_ref[:NB, :] = gram
        sum_ref[NB:, :] = jnp.where(flags_ref[0] == 1, panel[:NB], 0.0)

    @pl.when(i > 0)
    def _():
        sum_ref[:NB, :] += gram

    @pl.when(i == pl.num_programs(0) - 1)
    def _():
        share = 2 * NB // (N_ROW * N_COL)
        for r in range(N_ROW):
            for c in range(N_COL):
                to, of = (r * N_COL + c) * share, (c * N_ROW + r) * share
                left_ref[to : to + share, :] = sum_ref[of : of + share, :]
        strip = rows_of(b_ref, width)
        strip_ref[...] = strip
        right_ref[:NB, :] = dot(strip, strip, 1, 1)
        right_ref[NB:, :] = jnp.where(flags_ref[1] == 1, strip[:, strip.shape[1] - NB :].T, 0.0)


def grams(flags, araw, braw, rows_loc, cols_loc):
    width = cols_loc // LANES
    steps = rows_loc // TILE
    f32 = jnp.float32
    return pl.pallas_call(
        gram_kernel,
        out_shape=(
            jax.ShapeDtypeStruct((rows_loc, NB), f32),
            jax.ShapeDtypeStruct((NB, cols_loc), f32),
            jax.ShapeDtypeStruct((2 * NB, NB), f32),
            jax.ShapeDtypeStruct((2 * NB, NB), f32),
        ),
        grid_spec=pltpu.PrefetchScalarGridSpec(
            num_scalar_prefetch=1,
            grid=(steps,),
            in_specs=[
                pl.BlockSpec((TILE * width, LANES), lambda i, f: (i, 0)),
                pl.BlockSpec((NB * width, LANES), lambda i, f: (rows_loc // NB - 1, 0)),
            ],
            out_specs=[
                pl.BlockSpec((TILE, NB), lambda i, f: (i, 0)),
                pl.BlockSpec((NB, cols_loc), lambda i, f: (0, 0)),
                pl.BlockSpec((2 * NB, NB), lambda i, f: (0, 0)),
                pl.BlockSpec((2 * NB, NB), lambda i, f: (0, 0)),
            ],
            scratch_shapes=[pltpu.VMEM((2 * NB, NB), f32)],
        ),
        compiler_params=pltpu.CompilerParams(vmem_limit_bytes=60 * 2**20),
        cost_estimate=pl.CostEstimate(flops=2 * 10**9, bytes_accessed=6 * 10**6, transcendentals=0),
    )(flags, araw, braw)


def product_kernel(a_ref, b_ref, panel_ref, strip_ref, left_ref, right_ref, top_ref, end_ref, s_ref):
    i = pl.program_id(0)
    cols_loc = strip_ref.shape[1]
    width = cols_loc // LANES

    @pl.when(i == 0)
    def _():
        high, low = halves(strip_ref[...])
        s_ref[0] = high
        s_ref[1] = low

    strip = (s_ref[0], s_ref[1])
    panel = halves(panel_ref[...])
    for m, ref in enumerate((a_ref, b_ref)):
        whole = rows_of(ref, width)
        x = halves(whole)
        right_ref[m] = dot3(x, strip, 1, 1)
        end_ref[m] = whole[:, cols_loc - NB :]
        part = dot3(panel, x, 0, 0)
        at = slice(m * cols_loc, (m + 1) * cols_loc)

        @pl.when(i == 0)
        def _():
            left_ref[:, at] = part
            top_ref[:, at] = whole[:NB]

        @pl.when(i > 0)
        def _():
            left_ref[:, at] += part


def products(araw, braw, panel, strip):
    rows_loc, cols_loc = panel.shape[0], strip.shape[1]
    width = cols_loc // LANES
    f32 = jnp.float32
    raw = pl.BlockSpec((TILE * width, LANES), lambda i: (i, 0))
    wide = pl.BlockSpec((NB, 2 * cols_loc), lambda i: (0, 0))
    tall = pl.BlockSpec((2, TILE, NB), lambda i: (0, i, 0))
    return pl.pallas_call(
        product_kernel,
        grid=(rows_loc // TILE,),
        out_shape=(
            jax.ShapeDtypeStruct((NB, 2 * cols_loc), f32),
            jax.ShapeDtypeStruct((2, rows_loc, NB), f32),
            jax.ShapeDtypeStruct((NB, 2 * cols_loc), f32),
            jax.ShapeDtypeStruct((2, rows_loc, NB), f32),
        ),
        in_specs=[raw, raw, pl.BlockSpec((TILE, NB), lambda i: (i, 0)), pl.BlockSpec((NB, cols_loc), lambda i: (0, 0))],
        out_specs=(wide, tall, wide, tall),
        scratch_shapes=[pltpu.VMEM((2, NB, cols_loc), jnp.bfloat16)],
        compiler_params=pltpu.CompilerParams(vmem_limit_bytes=48 * 2**20),
        cost_estimate=pl.CostEstimate(flops=75 * 10**8, bytes_accessed=24 * 10**6, transcendentals=0),
    )(araw, braw, panel, strip)


def update_kernel(flags_ref, a_ref, b_ref, panel_ref, mixed_ref, la_ref, lb_ref, ta_ref, tb_ref, strip_ref, oa_ref, ob_ref, w_ref):
    i = pl.program_id(0)
    cols_loc = strip_ref.shape[1]
    width = cols_loc // LANES

    @pl.when(i == 0)
    def _():
        zh, zl = halves(strip_ref[...])
        for m, lift in enumerate((la_ref, lb_ref)):
            lh, ll = halves(lift[...])
            w_ref[0, m, :NB, :] = lh
            w_ref[1, m, :NB, :] = ll
            w_ref[0, m, NB:, :] = zh
            w_ref[1, m, NB:, :] = zl

    panel = panel_ref[...]
    on_top = (i == 0) & (flags_ref[0] == 1)
    for m, (ref, top_ref, out) in enumerate(((a_ref, ta_ref, oa_ref), (b_ref, tb_ref, ob_ref))):
        both = halves(jnp.concatenate([panel, mixed_ref[m]], axis=1))
        delta = dot3(both, (w_ref[0, m], w_ref[1, m]))
        for t in range(width):
            lanes = slice(t * LANES, (t + 1) * LANES)
            line = pl.ds(t, TILE, stride=width)
            out[line, :] = ref[line, :] - delta[:, lanes]

        @pl.when(on_top)
        def _():
            for t in range(width):
                line = pl.ds(t, NB, stride=width)
                lanes = slice(t * LANES, (t + 1) * LANES)
                out[line, :] = out[line, :] - top_ref[:, lanes]


def updated(flags, araw, braw, panel, mixed, lifts, tops, vectors_t):
    rows_loc, cols_loc = panel.shape[0], vectors_t.shape[1]
    width = cols_loc // LANES
    raw = pl.BlockSpec((TILE * width, LANES), lambda i, f: (i, 0))
    wide = pl.BlockSpec((NB, cols_loc), lambda i, f: (0, 0))
    return pl.pallas_call(
        update_kernel,
        out_shape=(jax.ShapeDtypeStruct(araw.shape, jnp.float32),) * 2,
        grid_spec=pltpu.PrefetchScalarGridSpec(
            num_scalar_prefetch=1,
            grid=(rows_loc // TILE,),
            in_specs=[
                raw,
                raw,
                pl.BlockSpec((TILE, NB), lambda i, f: (i, 0)),
                pl.BlockSpec((2, TILE, NB), lambda i, f: (0, i, 0)),
                *[wide] * 5,
            ],
            out_specs=[raw, raw],
            scratch_shapes=[pltpu.VMEM((2, 2, 2 * NB, cols_loc), jnp.bfloat16)],
        ),
        compiler_params=pltpu.CompilerParams(vmem_limit_bytes=60 * 2**20),
        cost_estimate=pl.CostEstimate(flops=75 * 10**8, bytes_accessed=28 * 10**6, transcendentals=0),
    )(flags, araw, braw, panel, mixed, *lifts, *tops, vectors_t)


X, Y = ("col", 4, 4), ("col", 1, 4)


def shifted(array, ring, step):
    axis, stride, size = ring
    hop = [((i // stride) % size, i) for i in range(lax.axis_size(axis))]
    return lax.ppermute(array, axis, [(i, i + ((p + step) % size - p) * stride) for p, i in hop])


def ring_total(array, ring):
    total = array
    for step in range(1, ring[2]):
        total = total + shifted(array, ring, step)
    return total


def after(array, *others):
    for other in others:
        array = array + 0.0 * other[(0,) * other.ndim]
    return array


def matmul(left, right, dims=((1,), (0,)), precision=lax.Precision.HIGH):
    return lax.dot_general(left, right, (dims, ((), ())), precision=precision, preferred_element_type=jnp.float32)


def exchanged(array, axis):
    return lax.all_to_all(array, axis, 0, 0, tiled=True)


def from_everyone(part, axis):
    return exchanged(jnp.broadcast_to(part, (lax.axis_size(axis), *part.shape)), axis)


def on_device(pencil_a, pencil_b):
    rows_loc = pencil_a.shape[1]
    cols_loc = pencil_a.shape[3]
    araw = pencil_a.reshape(-1, LANES)
    braw = pencil_b.reshape(-1, LANES)
    row, col = lax.axis_index("row"), lax.axis_index("col")
    n_row, n_col = lax.axis_size("row"), lax.axis_size("col")
    is_top, is_end = row == 0, col == n_col - 1
    flags = jnp.stack([is_top, is_end]).astype(jnp.int32)
    across, both = ((1,), (1,)), ((0,), (0,))
    panel, strip, left_sum, right_sum = grams(flags, araw, braw, rows_loc, cols_loc)
    folded = cols_loc // NB
    pieces = [strip[:, i * NB : (i + 1) * NB] for i in range(folded)]
    got = exchanged(jnp.concatenate([x.reshape(n_row, -1, NB) for x in [left_sum, *pieces]], axis=1), "row")
    half = 2 * NB // n_row
    strip = got[n_row - 1, half:]
    blocks = [panel, right_sum, jnp.sum(got[:, :half], axis=0)]
    got = exchanged(jnp.concatenate([x.reshape(n_col, -1, NB) for x in blocks], axis=1), "col")
    cut, end_cut = rows_loc // n_col, (rows_loc + 2 * NB) // n_col
    panel = from_everyone(got[0, :cut], "col").reshape(rows_loc, NB)
    everyone = lax.all_gather(jnp.concatenate([strip, jnp.sum(got[:, cut:end_cut], axis=0), got[0, end_cut:]]), "row")
    strip, everyone = everyone[:, : strip.shape[0]], everyone[:, strip.shape[0] :]
    strip = jnp.concatenate(
        [strip[:, i * NB // n_row : (i + 1) * NB // n_row].reshape(NB, NB) for i in range(folded)], axis=1
    )
    left_sum = everyone[:, end_cut - cut :].reshape(-1, NB)
    part = jnp.concatenate([everyone[n_row - 1, : end_cut - cut], left_sum])
    got = from_everyone(after(part, panel), "col")
    left, right, top, end = products(araw, braw, panel, strip)
    linv = inverses(lower_kernel, got, left, pl.BlockSpec(memory_space=pl.ANY))
    minv = inverses(general_kernel, got, linv, VMEM)
    right = matmul(right.reshape(2 * rows_loc, NB), linv[1], across)
    right = right + jnp.where(is_end, end.reshape(2 * rows_loc, NB), 0.0)
    left = lax.psum(matmul(linv[0], left) + jnp.where(is_top, top, 0.0), "row")
    right = jnp.sum(exchanged(right.reshape(n_col, -1, NB), "col"), axis=0)
    early = right
    right = from_everyone(right, "col")
    left = [left[:, :cols_loc], left[:, cols_loc:]]
    unit = jnp.eye(NB, dtype=jnp.float32)
    vectors_t = matmul(linv[1], strip)
    vectors_t = vectors_t + jnp.where(is_end, jnp.pad(unit, ((0, 0), (cols_loc - NB, 0))), 0.0)
    share = NB // n_row
    mine = after(lax.dynamic_slice_in_dim(vectors_t, row * share, share), minv, early)
    cross = jnp.concatenate([matmul(mine, left[0], across), matmul(mine, left[1], across)])
    cross = ring_total(ring_total(cross, X), Y)
    cross = lax.all_gather(matmul(cross, minv[0], across), "row").reshape(n_row, 2, share, NB)
    mixer = matmul(minv[1], vectors_t, both)
    lines, lifts = [], []
    for m in range(2):
        line = matmul(minv[0], left[m]) - matmul(cross[:, m].reshape(NB, NB), mixer, both)
        lines.append(line)
        lifts.append(matmul(linv[0], line, both))
    new_a, new_b = updated(flags, araw, braw, panel, right.reshape(2, rows_loc, NB), lifts, lines, mixer)
    return new_a.reshape(pencil_a.shape), new_b.reshape(pencil_b.shape)


def solution(mesh):
    placed = (P("row", None, "col", None), P("row", None, "col", None))
    return jax.shard_map(on_device, mesh=mesh, in_specs=placed, out_specs=placed, check_vma=False)
```

```python
import jax
import jax.numpy as jnp
from jax import lax
from jax.experimental import pallas as pl
from jax.experimental.pallas import tpu as pltpu
from jax.sharding import PartitionSpec as P

NB = 256
LEAF = 64
LANES = 128
TILE = 256
N_ROW = 8
N_COL = 16
VMEM = pl.BlockSpec(memory_space=pltpu.VMEM)


def dot(a, b, ca=1, cb=0):
    return lax.dot_general(a, b, (((ca,), (cb,)), ((), ())), precision=lax.Precision.HIGHEST,
                           preferred_element_type=jnp.float32)

PB = 4

def leaf_inverse(tiles, forward):
    n = len(tiles)
    wide = (8, 2 * LEAF)
    rows = lax.broadcasted_iota(jnp.int32, (LEAF, LEAF), 0)
    cols = lax.broadcasted_iota(jnp.int32, (LEAF, LEAF), 1)
    eye = (rows == cols).astype(jnp.float32)
    row_id = lax.broadcasted_iota(jnp.int32, wide, 0)
    full = [jnp.concatenate([t, eye], axis=1) for t in tiles]
    groups = LEAF // 8
    work = [[f[8 * g : 8 * g + 8] for g in range(groups)] for f in full]
    for j in range(0, LEAF, PB):
        own, at = j // 8, j % 8
        for m in range(n):
            w = work[m]
            touched = range(own, groups) if forward else range(groups)
            columns = {g: [jnp.broadcast_to(w[g][:, j + b : j + b + 1], wide) for b in range(PB)] for g in touched}
            band = [jnp.broadcast_to(w[own][at + a : at + a + 1, :], wide) for a in range(PB)]
            d = [[jnp.broadcast_to(columns[own][b][at + a : at + a + 1, :], wide) for b in range(PB)] for a in range(PB)]
            inv = []
            for k in range(PB):
                inv.append(1.0 / d[k][k])
                for a in range(k + 1, PB):
                    ratio = d[a][k] * inv[k]
                    for b in range(k + 1, PB):
                        d[a][b] = d[a][b] - ratio * d[k][b]
                    band[a] = band[a] - ratio * band[k]
            solved = list(band)
            if not forward:
                for a in reversed(range(PB)):
                    for b in range(a + 1, PB):
                        solved[a] = solved[a] - d[a][b] * solved[b]
                    solved[a] = solved[a] * inv[a]
            for g in touched:
                total = w[g]
                c = []
                for b in range(PB):
                    v = columns[g][b]
                    for k in range(b):
                        v = v - c[k] * d[k][b]
                    c.append(v * inv[b])
                    total = total - c[b] * band[b]
                if g == own:
                    if forward:
                        total = jnp.where(row_id < at, w[g], total)
                    for a in range(PB):
                        total = jnp.where(row_id == at + a, solved[a], total)
                w[g] = total
    out = []
    for m in range(n):
        f = jnp.concatenate(work[m], axis=0)
        left, right = f[:, :LEAF], f[:, LEAF:]
        if forward:
            dd = jnp.sum(jnp.where(rows == cols, left, 0.0), axis=1, keepdims=True)
            right = right * lax.rsqrt(dd)
        out.append(right)
    return out

def load(got_ref, m, first, w_ref):
    share = got_ref.shape[1] // 2
    lanes = (1 - m) * share
    for c in range(NB // share):
        w_ref[m, c * share : (c + 1) * share, :NB] = got_ref[first // share + c, lanes : lanes + share, :]


def lower_kernel(got_ref, _, out_ref, w_ref):
    rows = lax.broadcasted_iota(jnp.int32, (NB, NB), 0)
    cols = lax.broadcasted_iota(jnp.int32, (NB, NB), 1)
    steps = NB // LEAF
    for m in range(2):
        load(got_ref, m, 0, w_ref)
        w_ref[m, :, NB:] = (rows == cols).astype(jnp.float32)
    for k in range(steps):
        lo, hi = k * LEAF, (k + 1) * LEAF
        inv = leaf_inverse([w_ref[m, lo:hi, lo:hi] for m in range(2)], True)
        for m in range(2):
            band = dot(inv[m], w_ref[m, lo:hi, :])
            w_ref[m, lo:hi, :] = band
            if k < steps - 1:
                w_ref[m, hi:, :] = w_ref[m, hi:, :] - dot(band[:, hi:NB], band, 0, 0)
    for m in range(2):
        out_ref[m] = w_ref[m, :, NB:]


def general_kernel(got_ref, linv_ref, out_ref, w_ref):
    rows = lax.broadcasted_iota(jnp.int32, (NB, NB), 0)
    cols = lax.broadcasted_iota(jnp.int32, (NB, NB), 1)
    eye = (rows == cols).astype(jnp.float32)
    for m in range(2):
        load(got_ref, m, NB, w_ref)
        w_ref[m, :, :NB] = eye + dot(w_ref[m, :, :NB], linv_ref[m], 1, 1)
        w_ref[m, :, NB:] = eye
    for k in range(NB // LEAF):
        lo, hi = k * LEAF, (k + 1) * LEAF
        inv = leaf_inverse([w_ref[m, lo:hi, lo:hi] for m in range(2)], False)
        for m in range(2):
            band = dot(inv[m], w_ref[m, lo:hi, :])
            whole = w_ref[m]
            w_ref[m] = whole - dot(whole[:, lo:hi], band)
            w_ref[m, lo:hi, :] = band
    for m in range(2):
        out_ref[m] = w_ref[m, :, NB:]


def inverses(kernel, got, other, other_spec):
    return pl.pallas_call(
        kernel,
        out_shape=jax.ShapeDtypeStruct((2, NB, NB), jnp.float32),
        in_specs=[VMEM, other_spec],
        out_specs=VMEM,
        scratch_shapes=[pltpu.VMEM((2, NB, 2 * NB), jnp.float32)],
        compiler_params=pltpu.CompilerParams(vmem_limit_bytes=24 * 2**20),
        cost_estimate=pl.CostEstimate(flops=2 * 10**10, bytes_accessed=2 * 10**6, transcendentals=0),
    )(got, other)


def halves(x):
    high = x.astype(jnp.bfloat16)
    return high, (x - high.astype(jnp.float32)).astype(jnp.bfloat16)


def dot3(a, b, ca=1, cb=0):
    dims = (((ca,), (cb,)), ((), ()))

    def one(left, right):
        return lax.dot_general(left, right, dims, preferred_element_type=jnp.float32)

    return one(a[0], b[0]) + (one(a[0], b[1]) + one(a[1], b[0]))


def rows_of(ref, width, first=0, count=None):
    count = width if count is None else count
    height = ref.shape[0] // width
    return jnp.concatenate([ref[pl.ds(first + t, height, stride=width), :] for t in range(count)], axis=1)


def gram_kernel(flags_ref, a_ref, b_ref, first_ref, panel_ref, strip_ref, left_ref, right_ref, top_ref, sum_ref):
    i = pl.program_id(0)
    width = strip_ref.shape[1] // LANES
    panel = rows_of(a_ref, width, 0, NB // LANES)
    panel_ref[...] = panel
    gram = dot(panel, panel, 0, 0)

    @pl.when(i == 0)
    def _():
        sum_ref[:NB, :] = gram
        sum_ref[NB:, :] = jnp.where(flags_ref[0] == 1, panel[:NB], 0.0)
        cols_loc = strip_ref.shape[1]
        top_ref[:cols_loc, :] = rows_of(a_ref, width).T
        top_ref[cols_loc:, :] = rows_of(first_ref, width).T

    @pl.when(i > 0)
    def _():
        sum_ref[:NB, :] += gram

    @pl.when(i == pl.num_programs(0) - 1)
    def _():
        share = 2 * NB // (N_ROW * N_COL)
        for r in range(N_ROW):
            for c in range(N_COL):
                to, of = (r * N_COL + c) * share, (c * N_ROW + r) * share
                left_ref[to : to + share, :] = sum_ref[of : of + share, :]
        strip = rows_of(b_ref, width)
        strip_ref[...] = strip
        right_ref[:NB, :] = dot(strip, strip, 1, 1)
        right_ref[NB:, :] = jnp.where(flags_ref[1] == 1, strip[:, strip.shape[1] - NB :].T, 0.0)


def grams(flags, araw, braw, rows_loc, cols_loc):
    width = cols_loc // LANES
    steps = rows_loc // TILE
    f32 = jnp.float32
    return pl.pallas_call(
        gram_kernel,
        out_shape=(
            jax.ShapeDtypeStruct((rows_loc, NB), f32),
            jax.ShapeDtypeStruct((NB, cols_loc), f32),
            jax.ShapeDtypeStruct((2 * NB, NB), f32),
            jax.ShapeDtypeStruct((2 * NB, NB), f32),
            jax.ShapeDtypeStruct((2 * cols_loc, NB), f32),
        ),
        grid_spec=pltpu.PrefetchScalarGridSpec(
            num_scalar_prefetch=1,
            grid=(steps,),
            in_specs=[
                pl.BlockSpec((TILE * width, LANES), lambda i, f: (i, 0)),
                pl.BlockSpec((NB * width, LANES), lambda i, f: (rows_loc // NB - 1, 0)),
                pl.BlockSpec((NB * width, LANES), lambda i, f: (0, 0)),
            ],
            out_specs=[
                pl.BlockSpec((TILE, NB), lambda i, f: (i, 0)),
                pl.BlockSpec((NB, cols_loc), lambda i, f: (0, 0)),
                pl.BlockSpec((2 * NB, NB), lambda i, f: (0, 0)),
                pl.BlockSpec((2 * NB, NB), lambda i, f: (0, 0)),
                pl.BlockSpec((2 * cols_loc, NB), lambda i, f: (0, 0)),
            ],
            scratch_shapes=[pltpu.VMEM((2 * NB, NB), f32)],
        ),
        compiler_params=pltpu.CompilerParams(vmem_limit_bytes=60 * 2**20),
        cost_estimate=pl.CostEstimate(flops=2 * 10**9, bytes_accessed=6 * 10**6, transcendentals=0),
    )(flags, araw, braw, braw)


def product_kernel(a_ref, b_ref, panel_ref, strip_ref, left_ref, right_ref, end_ref, s_ref, sum_ref):
    i = pl.program_id(0)
    cols_loc = strip_ref.shape[1]
    width = cols_loc // LANES

    @pl.when(i == 0)
    def _():
        high, low = halves(strip_ref[...])
        s_ref[0] = high
        s_ref[1] = low
        sum_ref[...] = jnp.zeros_like(sum_ref)

    strip = (s_ref[0], s_ref[1])
    panel = halves(panel_ref[...])
    for m, ref in enumerate((a_ref, b_ref)):
        whole = rows_of(ref, width)
        x = halves(whole)
        right_ref[m] = dot3(x, strip, 1, 1)
        end_ref[m] = whole[:, cols_loc - NB :]
        sum_ref[:, m * cols_loc : (m + 1) * cols_loc] += dot3(panel, x, 0, 0)

    @pl.when(i == pl.num_programs(0) - 1)
    def _():
        left_ref[...] = sum_ref[...].T


def products(araw, braw, panel, strip):
    rows_loc, cols_loc = panel.shape[0], strip.shape[1]
    width = cols_loc // LANES
    f32 = jnp.float32
    raw = pl.BlockSpec((TILE * width, LANES), lambda i: (i, 0))
    tall = pl.BlockSpec((2, TILE, NB), lambda i: (0, i, 0))
    return pl.pallas_call(
        product_kernel,
        grid=(rows_loc // TILE,),
        out_shape=(
            jax.ShapeDtypeStruct((2 * cols_loc, NB), f32),
            jax.ShapeDtypeStruct((2, rows_loc, NB), f32),
            jax.ShapeDtypeStruct((2, rows_loc, NB), f32),
        ),
        in_specs=[raw, raw, pl.BlockSpec((TILE, NB), lambda i: (i, 0)), pl.BlockSpec((NB, cols_loc), lambda i: (0, 0))],
        out_specs=(pl.BlockSpec((2 * cols_loc, NB), lambda i: (0, 0)), tall, tall),
        scratch_shapes=[pltpu.VMEM((2, NB, cols_loc), jnp.bfloat16), pltpu.VMEM((NB, 2 * cols_loc), f32)],
        compiler_params=pltpu.CompilerParams(vmem_limit_bytes=48 * 2**20),
        cost_estimate=pl.CostEstimate(flops=75 * 10**8, bytes_accessed=22 * 10**6, transcendentals=0),
    )(araw, braw, panel, strip)


def update_kernel(flags_ref, a_ref, b_ref, panel_ref, mixed_ref, la_ref, lb_ref, ta_ref, tb_ref, strip_ref, oa_ref, ob_ref, w_ref):
    i = pl.program_id(0)
    cols_loc = strip_ref.shape[1]
    width = cols_loc // LANES

    @pl.when(i == 0)
    def _():
        zh, zl = halves(strip_ref[...])
        for m, lift in enumerate((la_ref, lb_ref)):
            lh, ll = halves(lift[...])
            w_ref[0, m, :NB, :] = lh
            w_ref[1, m, :NB, :] = ll
            w_ref[0, m, NB:, :] = zh
            w_ref[1, m, NB:, :] = zl

    panel = panel_ref[...]
    on_top = (i == 0) & (flags_ref[0] == 1)
    for m, (ref, top_ref, out) in enumerate(((a_ref, ta_ref, oa_ref), (b_ref, tb_ref, ob_ref))):
        both = halves(jnp.concatenate([panel, mixed_ref[m]], axis=1))
        delta = dot3(both, (w_ref[0, m], w_ref[1, m]))
        for t in range(width):
            lanes = slice(t * LANES, (t + 1) * LANES)
            line = pl.ds(t, TILE, stride=width)
            out[line, :] = ref[line, :] - delta[:, lanes]

        @pl.when(on_top)
        def _():
            for t in range(width):
                line = pl.ds(t, NB, stride=width)
                lanes = slice(t * LANES, (t + 1) * LANES)
                out[line, :] = out[line, :] - top_ref[:, lanes]


def updated(flags, araw, braw, panel, mixed, lifts, tops, vectors_t):
    rows_loc, cols_loc = panel.shape[0], vectors_t.shape[1]
    width = cols_loc // LANES
    raw = pl.BlockSpec((TILE * width, LANES), lambda i, f: (i, 0))
    wide = pl.BlockSpec((NB, cols_loc), lambda i, f: (0, 0))
    return pl.pallas_call(
        update_kernel,
        out_shape=(jax.ShapeDtypeStruct(araw.shape, jnp.float32),) * 2,
        grid_spec=pltpu.PrefetchScalarGridSpec(
            num_scalar_prefetch=1,
            grid=(rows_loc // TILE,),
            in_specs=[
                raw,
                raw,
                pl.BlockSpec((TILE, NB), lambda i, f: (i, 0)),
                pl.BlockSpec((2, TILE, NB), lambda i, f: (0, i, 0)),
                *[wide] * 5,
            ],
            out_specs=[raw, raw],
            scratch_shapes=[pltpu.VMEM((2, 2, 2 * NB, cols_loc), jnp.bfloat16)],
        ),
        compiler_params=pltpu.CompilerParams(vmem_limit_bytes=60 * 2**20),
        cost_estimate=pl.CostEstimate(flops=75 * 10**8, bytes_accessed=28 * 10**6, transcendentals=0),
    )(flags, araw, braw, panel, mixed, *lifts, *tops, vectors_t)


X, Y = ("col", 4, 4), ("col", 1, 4)


def shifted(array, ring, step):
    axis, stride, size = ring
    hop = [((i // stride) % size, i) for i in range(lax.axis_size(axis))]
    return lax.ppermute(array, axis, [(i, i + ((p + step) % size - p) * stride) for p, i in hop])


def ring_total(array, ring):
    total = array
    for step in range(1, ring[2]):
        total = total + shifted(array, ring, step)
    return total


def top_share(array):
    row = lax.axis_index("row")
    parts = array.reshape(4, 2, -1, array.shape[1])
    half = jnp.where(row == 1, lax.ppermute(parts[:, 1], "row", [(0, 1)]), parts[:, 0])
    share = jnp.where(row < 2, half[0], 0.0)
    for z in range(1, 4):
        share = share + lax.ppermute(half[z], "row", [(0, 2 * z), (1, 2 * z + 1)])
    return share


def after(array, *others):
    for other in others:
        array = array + 0.0 * other[(0,) * other.ndim]
    return array


def matmul(left, right, dims=((1,), (0,)), precision=lax.Precision.HIGH):
    return lax.dot_general(left, right, (dims, ((), ())), precision=precision, preferred_element_type=jnp.float32)


def exchanged(array, axis):
    return lax.all_to_all(array, axis, 0, 0, tiled=True)


def from_everyone(part, axis):
    return exchanged(jnp.broadcast_to(part, (lax.axis_size(axis), *part.shape)), axis)


def on_device(pencil_a, pencil_b):
    rows_loc = pencil_a.shape[1]
    cols_loc = pencil_a.shape[3]
    araw = pencil_a.reshape(-1, LANES)
    braw = pencil_b.reshape(-1, LANES)
    row, col = lax.axis_index("row"), lax.axis_index("col")
    n_row, n_col = lax.axis_size("row"), lax.axis_size("col")
    is_top, is_end = row == 0, col == n_col - 1
    flags = jnp.stack([is_top, is_end]).astype(jnp.int32)
    across, both = ((1,), (1,)), ((0,), (0,))
    panel, strip, left_sum, right_sum, top = grams(flags, araw, braw, rows_loc, cols_loc)
    folded = cols_loc // NB
    pieces = [strip[:, i * NB : (i + 1) * NB] for i in range(folded)]
    got = exchanged(jnp.concatenate([x.reshape(n_row, -1, NB) for x in [left_sum, *pieces]], axis=1), "row")
    half = 2 * NB // n_row
    strip = got[n_row - 1, half:]
    blocks = [panel, right_sum, jnp.sum(got[:, :half], axis=0)]
    got = exchanged(jnp.concatenate([x.reshape(n_col, -1, NB) for x in blocks], axis=1), "col")
    cut, end_cut = rows_loc // n_col, (rows_loc + 2 * NB) // n_col
    panel = from_everyone(got[0, :cut], "col").reshape(rows_loc, NB)
    everyone = lax.all_gather(jnp.concatenate([strip, jnp.sum(got[:, cut:end_cut], axis=0), got[0, end_cut:]]), "row")
    strip, everyone = everyone[:, : strip.shape[0]], everyone[:, strip.shape[0] :]
    strip = jnp.concatenate(
        [strip[:, i * NB // n_row : (i + 1) * NB // n_row].reshape(NB, NB) for i in range(folded)], axis=1
    )
    left_sum = everyone[:, end_cut - cut :].reshape(-1, NB)
    part = jnp.concatenate([everyone[n_row - 1, : end_cut - cut], left_sum])
    got = from_everyone(after(part, panel), "col")
    top = top_share(top)
    left, right, end = products(araw, braw, panel, strip)
    linv = inverses(lower_kernel, got, left, pl.BlockSpec(memory_space=pl.ANY))
    minv = inverses(general_kernel, got, linv, VMEM)
    right = matmul(right.reshape(2 * rows_loc, NB), linv[1], across)
    right = right + jnp.where(is_end, end.reshape(2 * rows_loc, NB), 0.0)
    left = jnp.sum(exchanged(left.reshape(n_row, -1, NB), "row"), axis=0)
    left = lax.all_gather(matmul(left, linv[0], across) + top, "row", tiled=True)
    right = jnp.sum(exchanged(right.reshape(n_col, -1, NB), "col"), axis=0)
    left = [left[:cols_loc], left[cols_loc:]]
    unit = jnp.eye(NB, dtype=jnp.float32)
    vectors_t = matmul(linv[1], strip)
    vectors_t = vectors_t + jnp.where(is_end, jnp.pad(unit, ((0, 0), (cols_loc - NB, 0))), 0.0)
    share = NB // n_row
    mine = after(lax.dynamic_slice_in_dim(vectors_t, row * share, share), minv)
    cross = jnp.concatenate([matmul(mine, left[0]), matmul(mine, left[1])])
    cross = ring_total(ring_total(cross, X), Y)
    right = from_everyone(after(right, cross), "col")
    cross = lax.all_gather(matmul(cross, minv[0], across), "row").reshape(n_row, 2, share, NB)
    mixer = matmul(minv[1], vectors_t, both)
    lines, lifts = [], []
    for m in range(2):
        line = matmul(minv[0], left[m], across) - matmul(cross[:, m].reshape(NB, NB), mixer, both)
        lines.append(line)
        lifts.append(matmul(linv[0], line, both))
    new_a, new_b = updated(flags, araw, braw, panel, right.reshape(2, rows_loc, NB), lifts, lines, mixer)
    return new_a.reshape(pencil_a.shape), new_b.reshape(pencil_b.shape)


def solution(mesh):
    placed = (P("row", None, "col", None), P("row", None, "col", None))
    return jax.shard_map(on_device, mesh=mesh, in_specs=placed, out_specs=placed, check_vma=False)
```

```python
import jax
import jax.numpy as jnp
from jax import lax
from jax.experimental import pallas as pl
from jax.experimental.pallas import tpu as pltpu
from jax.sharding import PartitionSpec as P

NB = 256
LEAF = 64
LANES = 128
TILE = 256
N_ROW = 8
N_COL = 16
VMEM = pl.BlockSpec(memory_space=pltpu.VMEM)


def dot(a, b, ca=1, cb=0):
    return lax.dot_general(a, b, (((ca,), (cb,)), ((), ())), precision=lax.Precision.HIGHEST,
                           preferred_element_type=jnp.float32)

PB = 4

def leaf_inverse(tiles, forward):
    n = len(tiles)
    wide = (8, 2 * LEAF)
    rows = lax.broadcasted_iota(jnp.int32, (LEAF, LEAF), 0)
    cols = lax.broadcasted_iota(jnp.int32, (LEAF, LEAF), 1)
    eye = (rows == cols).astype(jnp.float32)
    row_id = lax.broadcasted_iota(jnp.int32, wide, 0)
    full = [jnp.concatenate([t, eye], axis=1) for t in tiles]
    groups = LEAF // 8
    work = [[f[8 * g : 8 * g + 8] for g in range(groups)] for f in full]
    for j in range(0, LEAF, PB):
        own, at = j // 8, j % 8
        for m in range(n):
            w = work[m]
            touched = range(own, groups) if forward else range(groups)
            columns = {g: [jnp.broadcast_to(w[g][:, j + b : j + b + 1], wide) for b in range(PB)] for g in touched}
            band = [jnp.broadcast_to(w[own][at + a : at + a + 1, :], wide) for a in range(PB)]
            d = [[jnp.broadcast_to(columns[own][b][at + a : at + a + 1, :], wide) for b in range(PB)] for a in range(PB)]
            inv = []
            for k in range(PB):
                inv.append(1.0 / d[k][k])
                for a in range(k + 1, PB):
                    ratio = d[a][k] * inv[k]
                    for b in range(k + 1, PB):
                        d[a][b] = d[a][b] - ratio * d[k][b]
                    band[a] = band[a] - ratio * band[k]
            solved = list(band)
            if not forward:
                for a in reversed(range(PB)):
                    for b in range(a + 1, PB):
                        solved[a] = solved[a] - d[a][b] * solved[b]
                    solved[a] = solved[a] * inv[a]
            for g in touched:
                total = w[g]
                c = []
                for b in range(PB):
                    v = columns[g][b]
                    for k in range(b):
                        v = v - c[k] * d[k][b]
                    c.append(v * inv[b])
                    total = total - c[b] * band[b]
                if g == own:
                    if forward:
                        total = jnp.where(row_id < at, w[g], total)
                    for a in range(PB):
                        total = jnp.where(row_id == at + a, solved[a], total)
                w[g] = total
    out = []
    for m in range(n):
        f = jnp.concatenate(work[m], axis=0)
        left, right = f[:, :LEAF], f[:, LEAF:]
        if forward:
            dd = jnp.sum(jnp.where(rows == cols, left, 0.0), axis=1, keepdims=True)
            right = right * lax.rsqrt(dd)
        out.append(right)
    return out

def load(got_ref, m, first, w_ref):
    share = got_ref.shape[1] // 2
    lanes = (1 - m) * share
    for c in range(NB // share):
        w_ref[m, c * share : (c + 1) * share, :] = got_ref[first // share + c, lanes : lanes + share, :]


def lower_kernel(got_ref, _, out_ref, w_ref):
    rows = lax.broadcasted_iota(jnp.int32, (NB, NB), 0)
    cols = lax.broadcasted_iota(jnp.int32, (NB, NB), 1)
    steps = NB // LEAF
    eye = (rows[:LEAF, :LEAF] == cols[:LEAF, :LEAF]).astype(jnp.float32)
    for m in range(2):
        load(got_ref, m, 0, w_ref)
    for k in range(steps):
        lo, hi = k * LEAF, (k + 1) * LEAF
        inv = leaf_inverse([w_ref[m, lo:hi, lo:hi] for m in range(2)], True)
        for m in range(2):
            w_ref[m, lo:hi, lo:hi] = eye
            band = dot(inv[m], w_ref[m, lo:hi, :])
            w_ref[m, lo:hi, :] = band
            if k < steps - 1:
                w_ref[m, hi:, lo:hi] = jnp.zeros((NB - hi, LEAF), jnp.float32)
                w_ref[m, hi:, :] = w_ref[m, hi:, :] - dot(band[:, hi:NB], band, 0, 0)
    for m in range(2):
        out_ref[m] = jnp.where(rows >= cols, w_ref[m], 0.0)


def general_kernel(got_ref, linv_ref, out_ref, w_ref):
    rows = lax.broadcasted_iota(jnp.int32, (NB, NB), 0)
    cols = lax.broadcasted_iota(jnp.int32, (NB, NB), 1)
    eye = (rows == cols).astype(jnp.float32)
    for m in range(2):
        load(got_ref, m, NB, w_ref)
        w_ref[m] = eye + dot(w_ref[m], linv_ref[m], 1, 1)
    for k in range(NB // LEAF):
        lo, hi = k * LEAF, (k + 1) * LEAF
        inv = leaf_inverse([w_ref[m, lo:hi, lo:hi] for m in range(2)], False)
        for m in range(2):
            column = w_ref[m, :, lo:hi]
            w_ref[m, :, lo:hi] = jnp.zeros((NB, LEAF), jnp.float32)
            w_ref[m, lo:hi, lo:hi] = eye[:LEAF, :LEAF]
            band = dot(inv[m], w_ref[m, lo:hi, :])
            w_ref[m] = w_ref[m] - dot(column, band)
            w_ref[m, lo:hi, :] = band
    for m in range(2):
        out_ref[m] = w_ref[m]


def inverses(kernel, got, other, other_spec):
    return pl.pallas_call(
        kernel,
        out_shape=jax.ShapeDtypeStruct((2, NB, NB), jnp.float32),
        in_specs=[VMEM, other_spec],
        out_specs=VMEM,
        scratch_shapes=[pltpu.VMEM((2, NB, NB), jnp.float32)],
        compiler_params=pltpu.CompilerParams(vmem_limit_bytes=24 * 2**20),
        cost_estimate=pl.CostEstimate(flops=2 * 10**10, bytes_accessed=2 * 10**6, transcendentals=0),
    )(got, other)


def halves(x):
    high = x.astype(jnp.bfloat16)
    return high, (x - high.astype(jnp.float32)).astype(jnp.bfloat16)


def dot3(a, b, ca=1, cb=0):
    dims = (((ca,), (cb,)), ((), ()))

    def one(left, right):
        return lax.dot_general(left, right, dims, preferred_element_type=jnp.float32)

    return one(a[0], b[0]) + (one(a[0], b[1]) + one(a[1], b[0]))


def rows_of(ref, width, first=0, count=None):
    count = width if count is None else count
    height = ref.shape[0] // width
    return jnp.concatenate([ref[pl.ds(first + t, height, stride=width), :] for t in range(count)], axis=1)


def gram_kernel(flags_ref, a_ref, b_ref, first_ref, panel_ref, strip_ref, left_ref, right_ref, top_ref, sum_ref):
    i = pl.program_id(0)
    width = strip_ref.shape[1] // LANES
    panel = rows_of(a_ref, width, 0, NB // LANES)
    panel_ref[...] = panel
    gram = dot(panel, panel, 0, 0)

    @pl.when(i == 0)
    def _():
        sum_ref[:NB, :] = gram
        sum_ref[NB:, :] = jnp.where(flags_ref[0] == 1, panel[:NB], 0.0)
        cols_loc = strip_ref.shape[1]
        top_ref[:cols_loc, :] = rows_of(a_ref, width).T
        top_ref[cols_loc:, :] = rows_of(first_ref, width).T

    @pl.when(i > 0)
    def _():
        sum_ref[:NB, :] += gram

    @pl.when(i == pl.num_programs(0) - 1)
    def _():
        share = 2 * NB // (N_ROW * N_COL)
        for r in range(N_ROW):
            for c in range(N_COL):
                to, of = (r * N_COL + c) * share, (c * N_ROW + r) * share
                left_ref[to : to + share, :] = sum_ref[of : of + share, :]
        strip = rows_of(b_ref, width)
        strip_ref[...] = strip
        right_ref[:NB, :] = dot(strip, strip, 1, 1)
        right_ref[NB:, :] = jnp.where(flags_ref[1] == 1, strip[:, strip.shape[1] - NB :].T, 0.0)


def grams(flags, araw, braw, rows_loc, cols_loc):
    width = cols_loc // LANES
    steps = rows_loc // TILE
    f32 = jnp.float32
    return pl.pallas_call(
        gram_kernel,
        out_shape=(
            jax.ShapeDtypeStruct((rows_loc, NB), f32),
            jax.ShapeDtypeStruct((NB, cols_loc), f32),
            jax.ShapeDtypeStruct((2 * NB, NB), f32),
            jax.ShapeDtypeStruct((2 * NB, NB), f32),
            jax.ShapeDtypeStruct((2 * cols_loc, NB), f32),
        ),
        grid_spec=pltpu.PrefetchScalarGridSpec(
            num_scalar_prefetch=1,
            grid=(steps,),
            in_specs=[
                pl.BlockSpec((TILE * width, LANES), lambda i, f: (i, 0)),
                pl.BlockSpec((NB * width, LANES), lambda i, f: (rows_loc // NB - 1, 0)),
                pl.BlockSpec((NB * width, LANES), lambda i, f: (0, 0)),
            ],
            out_specs=[
                pl.BlockSpec((TILE, NB), lambda i, f: (i, 0)),
                pl.BlockSpec((NB, cols_loc), lambda i, f: (0, 0)),
                pl.BlockSpec((2 * NB, NB), lambda i, f: (0, 0)),
                pl.BlockSpec((2 * NB, NB), lambda i, f: (0, 0)),
                pl.BlockSpec((2 * cols_loc, NB), lambda i, f: (0, 0)),
            ],
            scratch_shapes=[pltpu.VMEM((2 * NB, NB), f32)],
        ),
        compiler_params=pltpu.CompilerParams(vmem_limit_bytes=60 * 2**20),
        cost_estimate=pl.CostEstimate(flops=2 * 10**9, bytes_accessed=6 * 10**6, transcendentals=0),
    )(flags, araw, braw, braw)


def product_kernel(a_ref, b_ref, panel_ref, strip_ref, left_ref, right_ref, end_ref, s_ref, sum_ref):
    i = pl.program_id(0)
    cols_loc = strip_ref.shape[1]
    width = cols_loc // LANES

    @pl.when(i == 0)
    def _():
        high, low = halves(strip_ref[...])
        s_ref[0] = high
        s_ref[1] = low
        sum_ref[...] = jnp.zeros_like(sum_ref)

    strip = (s_ref[0], s_ref[1])
    panel = halves(panel_ref[...])
    for m, ref in enumerate((a_ref, b_ref)):
        whole = rows_of(ref, width)
        x = halves(whole)
        right_ref[m] = dot3(x, strip, 1, 1)
        end_ref[m] = whole[:, cols_loc - NB :]
        sum_ref[:, m * cols_loc : (m + 1) * cols_loc] += dot3(panel, x, 0, 0)

    @pl.when(i == pl.num_programs(0) - 1)
    def _():
        left_ref[...] = sum_ref[...].T


def products(araw, braw, panel, strip):
    rows_loc, cols_loc = panel.shape[0], strip.shape[1]
    width = cols_loc // LANES
    f32 = jnp.float32
    raw = pl.BlockSpec((TILE * width, LANES), lambda i: (i, 0))
    tall = pl.BlockSpec((2, TILE, NB), lambda i: (0, i, 0))
    return pl.pallas_call(
        product_kernel,
        grid=(rows_loc // TILE,),
        out_shape=(
            jax.ShapeDtypeStruct((2 * cols_loc, NB), f32),
            jax.ShapeDtypeStruct((2, rows_loc, NB), f32),
            jax.ShapeDtypeStruct((2, rows_loc, NB), f32),
        ),
        in_specs=[raw, raw, pl.BlockSpec((TILE, NB), lambda i: (i, 0)), pl.BlockSpec((NB, cols_loc), lambda i: (0, 0))],
        out_specs=(pl.BlockSpec((2 * cols_loc, NB), lambda i: (0, 0)), tall, tall),
        scratch_shapes=[pltpu.VMEM((2, NB, cols_loc), jnp.bfloat16), pltpu.VMEM((NB, 2 * cols_loc), f32)],
        compiler_params=pltpu.CompilerParams(vmem_limit_bytes=48 * 2**20),
        cost_estimate=pl.CostEstimate(flops=75 * 10**8, bytes_accessed=22 * 10**6, transcendentals=0),
    )(araw, braw, panel, strip)


def update_kernel(flags_ref, a_ref, b_ref, panel_ref, mixed_ref, la_ref, lb_ref, ta_ref, tb_ref, strip_ref, oa_ref, ob_ref, w_ref):
    i = pl.program_id(0)
    cols_loc = strip_ref.shape[1]
    width = cols_loc // LANES

    @pl.when(i == 0)
    def _():
        zh, zl = halves(strip_ref[...])
        for m, lift in enumerate((la_ref, lb_ref)):
            lh, ll = halves(lift[...])
            w_ref[0, m, :NB, :] = lh
            w_ref[1, m, :NB, :] = ll
            w_ref[0, m, NB:, :] = zh
            w_ref[1, m, NB:, :] = zl

    panel = panel_ref[...]
    on_top = (i == 0) & (flags_ref[0] == 1)
    for m, (ref, top_ref, out) in enumerate(((a_ref, ta_ref, oa_ref), (b_ref, tb_ref, ob_ref))):
        both = halves(jnp.concatenate([panel, mixed_ref[m]], axis=1))
        delta = dot3(both, (w_ref[0, m], w_ref[1, m]))
        for t in range(width):
            lanes = slice(t * LANES, (t + 1) * LANES)
            line = pl.ds(t, TILE, stride=width)
            out[line, :] = ref[line, :] - delta[:, lanes]

        @pl.when(on_top)
        def _():
            for t in range(width):
                line = pl.ds(t, NB, stride=width)
                lanes = slice(t * LANES, (t + 1) * LANES)
                out[line, :] = out[line, :] - top_ref[:, lanes]


def updated(flags, araw, braw, panel, mixed, lifts, tops, vectors_t):
    rows_loc, cols_loc = panel.shape[0], vectors_t.shape[1]
    width = cols_loc // LANES
    raw = pl.BlockSpec((TILE * width, LANES), lambda i, f: (i, 0))
    wide = pl.BlockSpec((NB, cols_loc), lambda i, f: (0, 0))
    return pl.pallas_call(
        update_kernel,
        out_shape=(jax.ShapeDtypeStruct(araw.shape, jnp.float32),) * 2,
        grid_spec=pltpu.PrefetchScalarGridSpec(
            num_scalar_prefetch=1,
            grid=(rows_loc // TILE,),
            in_specs=[
                raw,
                raw,
                pl.BlockSpec((TILE, NB), lambda i, f: (i, 0)),
                pl.BlockSpec((2, TILE, NB), lambda i, f: (0, i, 0)),
                *[wide] * 5,
            ],
            out_specs=[raw, raw],
            scratch_shapes=[pltpu.VMEM((2, 2, 2 * NB, cols_loc), jnp.bfloat16)],
        ),
        compiler_params=pltpu.CompilerParams(vmem_limit_bytes=60 * 2**20),
        cost_estimate=pl.CostEstimate(flops=75 * 10**8, bytes_accessed=28 * 10**6, transcendentals=0),
    )(flags, araw, braw, panel, mixed, *lifts, *tops, vectors_t)


X, Y = ("col", 4, 4), ("col", 1, 4)


def shifted(array, ring, step):
    axis, stride, size = ring
    hop = [((i // stride) % size, i) for i in range(lax.axis_size(axis))]
    return lax.ppermute(array, axis, [(i, i + ((p + step) % size - p) * stride) for p, i in hop])


def ring_total(array, ring):
    total = array
    for step in range(1, ring[2]):
        total = total + shifted(array, ring, step)
    return total


def top_share(array):
    row = lax.axis_index("row")
    parts = array.reshape(4, 2, -1, array.shape[1])
    half = jnp.where(row == 1, lax.ppermute(parts[:, 1], "row", [(0, 1)]), parts[:, 0])
    share = jnp.where(row < 2, half[0], 0.0)
    for z in range(1, 4):
        share = share + lax.ppermute(half[z], "row", [(0, 2 * z), (1, 2 * z + 1)])
    return share


def after(array, *others):
    for other in others:
        array = array + 0.0 * other[(0,) * other.ndim]
    return array


def matmul(left, right, dims=((1,), (0,)), precision=lax.Precision.HIGH):
    return lax.dot_general(left, right, (dims, ((), ())), precision=precision, preferred_element_type=jnp.float32)


def exchanged(array, axis):
    return lax.all_to_all(array, axis, 0, 0, tiled=True)


def from_everyone(part, axis):
    return exchanged(jnp.broadcast_to(part, (lax.axis_size(axis), *part.shape)), axis)


def on_device(pencil_a, pencil_b):
    rows_loc = pencil_a.shape[1]
    cols_loc = pencil_a.shape[3]
    araw = pencil_a.reshape(-1, LANES)
    braw = pencil_b.reshape(-1, LANES)
    row, col = lax.axis_index("row"), lax.axis_index("col")
    n_row, n_col = lax.axis_size("row"), lax.axis_size("col")
    is_top, is_end = row == 0, col == n_col - 1
    flags = jnp.stack([is_top, is_end]).astype(jnp.int32)
    across, both = ((1,), (1,)), ((0,), (0,))
    panel, strip, left_sum, right_sum, top = grams(flags, araw, braw, rows_loc, cols_loc)
    folded = cols_loc // NB
    pieces = [strip[:, i * NB : (i + 1) * NB] for i in range(folded)]
    got = exchanged(jnp.concatenate([x.reshape(n_row, -1, NB) for x in [left_sum, *pieces]], axis=1), "row")
    half = 2 * NB // n_row
    strip = got[n_row - 1, half:]
    blocks = [panel, right_sum, jnp.sum(got[:, :half], axis=0)]
    got = exchanged(jnp.concatenate([x.reshape(n_col, -1, NB) for x in blocks], axis=1), "col")
    cut, end_cut = rows_loc // n_col, (rows_loc + 2 * NB) // n_col
    panel = from_everyone(got[0, :cut], "col").reshape(rows_loc, NB)
    everyone = lax.all_gather(jnp.concatenate([strip, jnp.sum(got[:, cut:end_cut], axis=0), got[0, end_cut:]]), "row")
    strip, everyone = everyone[:, : strip.shape[0]], everyone[:, strip.shape[0] :]
    strip = jnp.concatenate(
        [strip[:, i * NB // n_row : (i + 1) * NB // n_row].reshape(NB, NB) for i in range(folded)], axis=1
    )
    left_sum = everyone[:, end_cut - cut :].reshape(-1, NB)
    part = jnp.concatenate([everyone[n_row - 1, : end_cut - cut], left_sum])
    got = from_everyone(after(part, panel), "col")
    top = top_share(top)
    left, right, end = products(araw, braw, panel, strip)
    linv = inverses(lower_kernel, got, left, pl.BlockSpec(memory_space=pl.ANY))
    minv = inverses(general_kernel, got, linv, VMEM)
    right = matmul(right.reshape(2 * rows_loc, NB), linv[1], across)
    right = right + jnp.where(is_end, end.reshape(2 * rows_loc, NB), 0.0)
    left = jnp.sum(exchanged(left.reshape(n_row, -1, NB), "row"), axis=0)
    left = lax.all_gather(matmul(left, linv[0], across) + top, "row", tiled=True)
    right = jnp.sum(exchanged(right.reshape(n_col, -1, NB), "col"), axis=0)
    left = [left[:cols_loc], left[cols_loc:]]
    unit = jnp.eye(NB, dtype=jnp.float32)
    vectors_t = matmul(linv[1], strip)
    vectors_t = vectors_t + jnp.where(is_end, jnp.pad(unit, ((0, 0), (cols_loc - NB, 0))), 0.0)
    share = NB // n_row
    mine = after(lax.dynamic_slice_in_dim(vectors_t, row * share, share), minv)
    cross = jnp.concatenate([matmul(mine, left[0]), matmul(mine, left[1])])
    cross = ring_total(ring_total(cross, X), Y)
    right = from_everyone(after(right, cross), "col")
    cross = lax.all_gather(matmul(cross, minv[0], across), "row").reshape(n_row, 2, share, NB)
    mixer = matmul(minv[1], vectors_t, both)
    lines, lifts = [], []
    for m in range(2):
        line = matmul(minv[0], left[m], across) - matmul(cross[:, m].reshape(NB, NB), mixer, both)
        lines.append(line)
        lifts.append(matmul(linv[0], line, both))
    new_a, new_b = updated(flags, araw, braw, panel, right.reshape(2, rows_loc, NB), lifts, lines, mixer)
    return new_a.reshape(pencil_a.shape), new_b.reshape(pencil_b.shape)


def solution(mesh):
    placed = (P("row", None, "col", None), P("row", None, "col", None))
    return jax.shard_map(on_device, mesh=mesh, in_specs=placed, out_specs=placed, check_vma=False)
```
